1024 devices in a mesh: depth: 8 (over x), row: 8 (over y_lo, core), col: 16 (over y_hi, z).
Axes of the slice: x: 8, y: 8 (y_hi: 2, y_lo: 4; y = y_hi * 4 + y_lo), z: 8, core: 2. Of those that a mesh axis runs over, the one named last changes fastest.
Arguments:
- matrix_tiles: bfloat16 [2048, 256, 256], P(('depth', 'row', 'col')), may hold values from -3 to 3
- matrix_where: int32 [2048, 2], P(('depth', 'row', 'col')), may hold values from 0 to 511, as said below
- matrix_count: int32 [1024], P(('depth', 'row', 'col')), may hold values from 0 to 2, as said below
- square_tiles: bfloat16 [4096, 256, 256], P(('depth', 'row', 'col')), may hold values from -0.375 to 0.375
- square_where: int32 [4096, 2], P(('depth', 'row', 'col')), may hold values from 0 to 511, as said below
- square_count: int32 [1024], P(('depth', 'row', 'col')), may hold values from 0 to 4, as said below
Outputs:
- sign_step: float32 [2048, 4096], P('row', 'col')
The draws below stay inside these ranges and needn't reach their ends.
Inputs may be any that keep to these rules, and one draw needn't show every extreme that they name: `matrix_count`: among the devices that share a depth and a row index, at least one has exactly 2 live slots. `matrix_where`: every slot of the device at depth d, row r, col c names block row r and inner block d * 64 + c * 4 + s for some 0 <= s < 4; the slots of one device name distinct blocks. `square_count`: among the devices that share a depth and a col index, at least one has exactly 4 live slots. `square_where`: every slot of the device at depth d, row r, col c names inner block d * 64 + r * 8 + s for some 0 <= s < 8 and block column c; the slots of one device name distinct blocks.
All inputs are finite; a program needn't handle non-finite values.
Results may differ from the reference program's by a relative error of at most 0.0003.
Values may be sent and summed in bfloat16 or wider, within the bound.
No kernel may reach another device: no remote copies, remote signals or barrier semaphores. Data moves between devices by JAX's collectives and lax.ppermute only.
A program may use at most 64 MiB of HBM per device.

```python
import jax
import jax.numpy as jnp
from jax import lax

TILE = 256
KDEP = 64
XSLAB = 4
QSLAB = 8
XCAP = 2
QCAP = 4
N_DEPTH = 8
N_ROW = 8
N_COL = 16
DEVICES = 1024


def slab_slots(key, slab_size, keep_slots):
    scores = jax.random.randint(key, (DEVICES, slab_size), 0, 1 << 20) * slab_size + jnp.arange(slab_size, dtype=jnp.int32)[None, :]
    ordering = jnp.argsort(scores, axis=1, stable=True)
    return ordering[:, :keep_slots].astype(jnp.int32)


def skewed_counts(key, groups, members, largest):
    key_counts = jax.random.fold_in(key, 1)
    key_heavy = jax.random.fold_in(key, 2)
    counts = jax.random.randint(key_counts, (groups, members), 0, largest + 1)
    heavy_one = jax.random.randint(key_heavy, (groups,), 0, members)
    return jnp.where(jnp.arange(members, dtype=jnp.int32)[None, :] == heavy_one[:, None], largest, counts).astype(jnp.int32)


def device_indices():
    device = jnp.arange(DEVICES, dtype=jnp.int32)
    layer_idx = device // (N_ROW * N_COL)
    row_idx = device // N_COL % N_ROW
    col_idx = device % N_COL
    return (layer_idx, row_idx, col_idx)


def draw_matrix_where(key, part):
    key = jax.random.fold_in(key, 11)
    chosen = slab_slots(key, XSLAB, XCAP)
    layer_idx, row_idx, col_idx = device_indices()
    inner = layer_idx[:, None] * KDEP + col_idx[:, None] * XSLAB + chosen
    block_row = jnp.broadcast_to(row_idx[:, None], inner.shape)
    return jnp.stack([block_row, inner], axis=-1).reshape(DEVICES * XCAP, 2).astype(jnp.int32)


def draw_matrix_count(key, part):
    key = jax.random.fold_in(key, 12)
    counts = skewed_counts(key, N_DEPTH * N_ROW, N_COL, XCAP)
    return counts.reshape(DEVICES)


def draw_square_where(key, part):
    key = jax.random.fold_in(key, 13)
    chosen = slab_slots(key, QSLAB, QCAP)
    layer_idx, row_idx, col_idx = device_indices()
    inner = layer_idx[:, None] * KDEP + row_idx[:, None] * QSLAB + chosen
    block_col = jnp.broadcast_to(col_idx[:, None], inner.shape)
    return jnp.stack([inner, block_col], axis=-1).reshape(DEVICES * QCAP, 2).astype(jnp.int32)


def draw_square_count(key, part):
    key = jax.random.fold_in(key, 14)
    counts = skewed_counts(key, N_DEPTH * N_COL, N_ROW, QCAP)
    counts = counts.reshape(N_DEPTH, N_COL, N_ROW).transpose(0, 2, 1)
    return counts.reshape(DEVICES)


def shard_levels(key, shape, shards, smallest, top_value):
    level, own = 1.0, jax.random.fold_in(key, 6)
    for dim, shards_of in shards:
        heights = jnp.exp(jax.random.uniform(jax.random.fold_in(own, dim), (shards_of,), jnp.float32, smallest / len(shards), top_value / len(shards)))
        level = level * jnp.repeat(heights, shape[dim] // shards_of).reshape([-1 if axis == dim else 1 for axis in range(len(shape))])
    return level


def normal_values(own_key, shape, spread, bound, split=(), held_as=jnp.bfloat16):
    entries = jax.random.normal(own_key, shape, jnp.float32) * spread
    if len(split) > 0:
        entries = shard_levels(own_key, shape, split, -0.22, 0.18) * entries
    return jnp.clip(entries, min=-bound, max=bound).astype(held_as)


def setup_inputs(seed: int = 0) -> dict:
    splits = jax.random.split(jax.random.key(seed), 7)
    matrix_tiles = normal_values(splits[0], (DEVICES * XCAP, TILE, TILE), 0.5, 3.0, ((0, 1024),))
    matrix_where = draw_matrix_where(jax.random.fold_in(splits[6], 71), 0)
    matrix_count = draw_matrix_count(jax.random.fold_in(splits[6], 71), 0)
    square_tiles = normal_values(splits[3], (DEVICES * QCAP, TILE, TILE), 0.0625, 0.375, ((0, 1024),))
    square_where = draw_square_where(jax.random.fold_in(splits[6], 71), 0)
    square_count = draw_square_count(jax.random.fold_in(splits[6], 71), 0)
    return {"matrix_tiles": matrix_tiles, "matrix_where": matrix_where, "matrix_count": matrix_count, "square_tiles": square_tiles, "square_where": square_where, "square_count": square_count}


def place(tiles, live_slot, block_rows, block_cols, panel_rows, panel_cols):
    kept = tiles * live_slot[:, None, None].astype(tiles.dtype)
    panel = jnp.zeros((panel_rows, panel_cols, TILE, TILE), tiles.dtype)
    return panel.at[block_rows, block_cols].add(kept, mode="drop")


def as_matrix(panel):
    return panel.transpose(0, 2, 1, 3).reshape(panel.shape[0] * TILE, panel.shape[1] * TILE)


def reference(matrix_tiles, matrix_where, matrix_count, square_tiles, square_where, square_count):
    matrix_live = (jnp.arange(XCAP, dtype=jnp.int32)[None, :] < matrix_count[:, None]).reshape(-1)
    square_live = (jnp.arange(QCAP, dtype=jnp.int32)[None, :] < square_count[:, None]).reshape(-1)
    block_rows = matrix_where[:, 0].astype(jnp.int32)
    matrix_inner = matrix_where[:, 1].astype(jnp.int32)
    square_inner = square_where[:, 0].astype(jnp.int32)
    square_cols = square_where[:, 1].astype(jnp.int32)

    def layer_term(running, layer_idx):
        inner_base = layer_idx * KDEP
        matrix_pos = jnp.where((matrix_inner >= inner_base) & (matrix_inner < inner_base + KDEP), matrix_inner - inner_base, KDEP).astype(jnp.int32)
        square_pos = jnp.where((square_inner >= inner_base) & (square_inner < inner_base + KDEP), square_inner - inner_base, KDEP).astype(jnp.int32)
        left_side = as_matrix(place(matrix_tiles, matrix_live, block_rows, matrix_pos, N_ROW, KDEP)).astype(jnp.float32)
        right_side = as_matrix(place(square_tiles, square_live, square_pos, square_cols, KDEP, N_COL)).astype(jnp.float32)
        update = jnp.dot(left_side, right_side, precision=lax.Precision.HIGHEST, preferred_element_type=jnp.float32)
        return running + update, None

    start_sum = jnp.zeros((N_ROW * TILE, N_COL * TILE), jnp.float32)
    product, _ = lax.scan(layer_term, start_sum, jnp.arange(N_DEPTH, dtype=jnp.int32))
    diagonal_pos = jnp.where(matrix_inner < N_COL, matrix_inner, N_COL).astype(jnp.int32)
    diagonal_part = as_matrix(place(matrix_tiles, matrix_live, block_rows, diagonal_pos, N_ROW, N_COL)).astype(jnp.float32)
    return 1.5 * diagonal_part - 0.5 * product
```

```python
import functools

import jax
import jax.numpy as jnp
from jax import lax
from jax.experimental import pallas as pl
from jax.experimental.pallas import tpu as pltpu
from jax.sharding import PartitionSpec as P

TILE = 256
META = 16
MSG = 2 * TILE + META
KDEP = 64
XSLAB = 4
QSLAB = 8
ROW_COL = ("row", "col")


def flat(y, core, z):
    return ((y & 3) * 2 + core) * 16 + (y >> 2) * 8 + z


def places():
    return [(y, core, z) for y in range(8) for core in range(2) for z in range(8)]


def core_pairs():
    return [
        (flat(y, 1 - core, z), flat(y, core, z)) for y, core, z in places() if (z >> 1 & 1) == core
    ]


def swap_pairs():
    return [(flat(y, core, z), flat(y, 1 - core, z)) for y, core, z in places()]


def z_pairs(step, way):
    pairs = []
    for y, core, z in places():
        origin = (z - way * (step - 1)) % 8
        if (origin >> 1 & 1) == core:
            pairs.append((flat(y, core, z), flat(y, core, (z + way) % 8)))
    return pairs


def y_pairs(step, way, reach):
    pairs = []
    for y, core, z in places():
        origin = (y - way * (step - 1)) % 8
        ends = [(origin + way * t) % 8 for t in range(step, reach + 1)]
        if any((origin >> 1 & 1) == (end >> 2) for end in ends):
            pairs.append((flat(y, core, z), flat((y + way) % 8, core, z)))
    return pairs


def with_keys(tiles, keys):
    rows = jnp.broadcast_to(jnp.pad(keys, (0, META - 2), constant_values=-1)[:, None], (META, TILE))
    return jnp.concatenate([tiles.reshape(2 * TILE, TILE), rows.astype(jnp.bfloat16)], axis=0)


def product_kernel(*refs):
    x_refs, qa_refs, qb_refs = refs[:8], refs[8:16], refs[16:24]
    keep_ref, send_ref, x_buf, q_buf, key_vec, keys, x_sem, q_sem, key_sem = refs[24:]
    layer = lax.axis_index("depth")
    row_at = lax.axis_index("row")
    col_at = lax.axis_index("col")
    core = row_at & 1
    z = col_at & 7
    y_hi = col_at >> 3
    y = y_hi * 4 + (row_at >> 1)
    for d in range(8):
        origin = (z - d) & 7
        slot = (origin >> 2) * 2 + (origin & 1)

        @pl.when(((origin >> 1) & 1) == core)
        def _():
            pltpu.make_async_copy(x_refs[d], x_buf.at[slot], x_sem.at[slot]).start()

        source = (y - d) & 7
        place = (source >> 2) * 2 + (source & 1)

        @pl.when(((source >> 1) & 1) == y_hi)
        def _():
            pltpu.make_async_copy(qa_refs[d], q_buf.at[place, 0], q_sem.at[place, 0]).start()
            pltpu.make_async_copy(qb_refs[d], q_buf.at[place, 1], q_sem.at[place, 1]).start()

    keep_ref[...] = jnp.zeros_like(keep_ref)
    send_ref[...] = jnp.zeros_like(send_ref)
    for slot in range(4):
        pltpu.make_async_copy(x_refs[0], x_buf.at[slot], x_sem.at[slot]).wait()
        for half in range(2):
            pltpu.make_async_copy(qa_refs[0], q_buf.at[slot, half], q_sem.at[slot, half]).wait()

    lane = lax.broadcasted_iota(jnp.int32, (META, 128), 1)
    packed = jnp.zeros((META, 128), jnp.float32)
    for slot in range(4):
        for half in range(2):
            at = half * MSG + 2 * TILE
            x_rows = x_buf[slot, at : at + META, :128].astype(jnp.float32)
            q_rows = q_buf[slot, half, 2 * TILE :, :128].astype(jnp.float32)
            packed = jnp.where(lane == slot * 2 + half, x_rows, packed)
            packed = jnp.where(lane == 8 + slot * 2 + half, q_rows, packed)
    key_vec[...] = packed[:8].astype(jnp.int32)
    fetch = pltpu.make_async_copy(key_vec, keys, key_sem)
    fetch.start()
    fetch.wait()

    for h, out_ref in enumerate((keep_ref, send_ref)):

        def tile_step(i, carry, h=h, out_ref=out_ref):
            slot = i >> 1
            s = i & 1
            k4 = slot >> 1
            k2 = slot & 1
            key = keys[s, slot * 2 + h]
            inner = k2 * 4 + key
            start = pl.multiple_of(h * MSG + s * TILE, 16)
            for b in range(2):
                place = b * 2 + k4
                match = jnp.int32(-1)
                for j in range(4):
                    match = jnp.where(keys[j & 1, 8 + place * 2 + (j >> 1)] == inner, j, match)

                @pl.when((key >= 0) & (match >= 0))
                def _():
                    q_start = pl.multiple_of((match & 1) * TILE, 16)
                    out_ref[b] += jnp.dot(
                        x_buf[slot, pl.ds(start, TILE), :],
                        q_buf[place, match >> 1, pl.ds(q_start, TILE), :],
                        preferred_element_type=jnp.float32,
                    )

            @pl.when((key >= 0) & (layer == 0) & (y_hi == 0) & (k4 == 0) & (inner == z))
            def _():
                out_ref[core] -= 3.0 * x_buf[slot, pl.ds(start, TILE), :].astype(jnp.float32)

            return carry

        lax.fori_loop(0, 8, tile_step, 0)


def products(x_pieces, qa_pieces, qb_pieces):
    block = jax.ShapeDtypeStruct((2, TILE, TILE), jnp.float32)
    return pl.pallas_call(
        product_kernel,
        out_shape=(block, block),
        in_specs=[pl.BlockSpec(memory_space=pltpu.HBM)] * 24,
        out_specs=(pl.BlockSpec(memory_space=pltpu.VMEM),) * 2,
        scratch_shapes=[
            pltpu.VMEM((4, 2 * MSG, TILE), jnp.bfloat16),
            pltpu.VMEM((4, 2, MSG, TILE), jnp.bfloat16),
            pltpu.VMEM((8, 128), jnp.int32),
            pltpu.SMEM((8, 128), jnp.int32),
            pltpu.SemaphoreType.DMA((4,)),
            pltpu.SemaphoreType.DMA((4, 2)),
            pltpu.SemaphoreType.DMA,
        ],
        compiler_params=pltpu.CompilerParams(vmem_limit_bytes=24 * 1024 * 1024),
        cost_estimate=pl.CostEstimate(flops=2**28, bytes_accessed=5 * 2**20, transcendentals=0),
    )(*x_pieces, *qa_pieces, *qb_pieces)


def on_device(matrix_tiles, matrix_where, matrix_count, square_tiles, square_where, square_count):
    layer_at = lax.axis_index("depth")
    row_at = lax.axis_index("row")
    col_at = lax.axis_index("col")
    x_live = jnp.arange(2, dtype=jnp.int32) < matrix_count[0]
    q_live = jnp.arange(4, dtype=jnp.int32) < square_count[0]
    x_key = jnp.where(x_live, matrix_where[:, 1] - layer_at * KDEP - col_at * XSLAB, -1)
    q_key = jnp.where(q_live, square_where[:, 0] - layer_at * KDEP - row_at * QSLAB, -1)

    permute = functools.partial(lax.ppermute, axis_name=ROW_COL)
    with jax.named_scope("pack_matrix"):
        own_x = with_keys(matrix_tiles, x_key)
    with jax.named_scope("pair_matrix"):
        other_x = permute(own_x, perm=core_pairs())
        x_message = jnp.concatenate([own_x, other_x], axis=0)
    with jax.named_scope("pack_square"):
        qa = with_keys(square_tiles[:2], q_key[:2])
        qb = with_keys(square_tiles[2:], q_key[2:])

    x_pieces = [x_message] + [None] * 7
    qa_pieces = [qa] + [None] * 7
    qb_pieces = [qb] + [None] * 7
    right = [qa, qb, x_message]
    left = [qa, qb, x_message]
    for step in range(1, 5):
        with jax.named_scope("ring"):
            right[0] = permute(right[0], perm=y_pairs(step, 1, 4))
            qa_pieces[step] = right[0]
            if step < 4:
                left[0] = permute(left[0], perm=y_pairs(step, -1, 3))
                qa_pieces[8 - step] = left[0]
                right[1] = permute(right[1], perm=y_pairs(step, 1, 3))
                qb_pieces[step] = right[1]
            left[1] = permute(left[1], perm=y_pairs(step, -1, 4))
            qb_pieces[8 - step] = left[1]
            right[2] = permute(right[2], perm=z_pairs(step, 1))
            x_pieces[step] = right[2]
            if step < 4:
                left[2] = permute(left[2], perm=z_pairs(step, -1))
                x_pieces[8 - step] = left[2]

    keep, send = products(x_pieces, qa_pieces, qb_pieces)
    with jax.named_scope("pair_sum"):
        part = keep + permute(send, perm=swap_pairs())
    with jax.named_scope("scatter_sum"):
        groups = [
            [layer * 16 + y_hi * 8 + z for y_hi in range(2) for layer in range(8)] for z in range(8)
        ]
        shares = lax.all_to_all(
            part.reshape(16, TILE // 8, TILE), ("depth", "col"), 0, 0, axis_index_groups=groups
        )
        own = -0.5 * jnp.sum(shares, axis=0)
    with jax.named_scope("gather_rows"):
        spread = jnp.broadcast_to(own[None], (8, TILE // 8, TILE))
        return lax.all_to_all(spread, "depth", 0, 0).reshape(TILE, TILE)


def solution(mesh):
    in_specs = (
        P(("depth", "row", "col"), None, None),
        P(("depth", "row", "col"), None),
        P(("depth", "row", "col")),
        P(("depth", "row", "col"), None, None),
        P(("depth", "row", "col"), None),
        P(("depth", "row", "col")),
    )
    return jax.shard_map(
        on_device, mesh=mesh, in_specs=in_specs, out_specs=P("row", "col"), check_vma=False
    )
```

```python
import functools

import jax
import jax.numpy as jnp
from jax import lax
from jax.experimental import pallas as pl
from jax.experimental.pallas import tpu as pltpu
from jax.sharding import PartitionSpec as P

TILE = 256
META = 16
X_ROWS = 2 * TILE + META
Q_ROWS = 4 * TILE + META
KDEP = 64
XSLAB = 4
QSLAB = 8
ROW_COL = ("row", "col")


def flat(y, core, z):
    return ((y & 3) * 2 + core) * 16 + (y >> 2) * 8 + z


def places():
    return [(y, core, z) for y in range(8) for core in range(2) for z in range(8)]


def swap_pairs():
    return [(flat(y, core, z), flat(y, 1 - core, z)) for y, core, z in places()]


def z_pairs(step, way):
    pairs = []
    for y, core, z in places():
        origin = (z - way * (step - 1)) % 8
        if (origin >> 1 & 1) == core:
            pairs.append((flat(y, core, z), flat(y, core, (z + way) % 8)))
    return pairs


def needed(origin, target):
    return (origin >> 1 & 1) == (target >> 2)


def y_pairs(step, reach):
    pairs = []
    for y, core, z in places():
        way = 1 - 2 * core
        origin = (y - way * (step - 1)) % 8
        if any(needed(origin, (origin + way * t) % 8) for t in range(step, reach + 1)):
            pairs.append((flat(y, core, z), flat((y + way) % 8, core, z)))
    return pairs


def share_pairs(step):
    return [
        (flat(y, core, z), flat(y, 1 - core, z))
        for y, core, z in places()
        if needed((y - (1 - 2 * core) * step) % 8, y)
    ]


def with_keys(tiles, keys):
    count = tiles.shape[0]
    rows = jnp.pad(keys, (0, META - count), constant_values=-1)
    rows = jnp.broadcast_to(rows[:, None], (META, TILE)).astype(jnp.bfloat16)
    return jnp.concatenate([tiles.reshape(count * TILE, TILE), rows], axis=0)


def product_kernel(*refs):
    x_refs, q_refs = refs[:8], refs[8:16]
    keep_ref, send_ref, x_buf, q_buf, key_vec, keys, x_sem, q_sem, key_sem = refs[16:]
    layer = lax.axis_index("depth")
    row_at = lax.axis_index("row")
    col_at = lax.axis_index("col")
    core = row_at & 1
    z = col_at & 7
    y_hi = col_at >> 3
    y = y_hi * 4 + (row_at >> 1)
    for d in range(8):
        origin = (z - d) & 7
        slot = (origin >> 2) * 2 + (origin & 1)

        @pl.when(((origin >> 1) & 1) == core)
        def _():
            pltpu.make_async_copy(x_refs[d], x_buf.at[slot], x_sem.at[slot]).start()

        source = (y - (1 - 2 * core) * (d if d < 5 else 4 - d)) & 7
        place = (source >> 2) * 2 + (source & 1)

        @pl.when(((source >> 1) & 1) == y_hi)
        def _():
            pltpu.make_async_copy(q_refs[d], q_buf.at[place], q_sem.at[place]).start()

    keep_ref[...] = jnp.zeros_like(keep_ref)
    send_ref[...] = jnp.zeros_like(send_ref)
    for slot in range(4):
        pltpu.make_async_copy(x_refs[0], x_buf.at[slot], x_sem.at[slot]).wait()
        pltpu.make_async_copy(q_refs[0], q_buf.at[slot], q_sem.at[slot]).wait()

    lane = lax.broadcasted_iota(jnp.int32, (META, 128), 1)
    packed = jnp.zeros((META, 128), jnp.float32)
    for slot in range(4):
        for half in range(2):
            at = half * X_ROWS + 2 * TILE
            x_rows = x_buf[slot, at : at + META, :128].astype(jnp.float32)
            packed = jnp.where(lane == slot * 2 + half, x_rows, packed)
        q_rows = q_buf[slot, 4 * TILE :, :128].astype(jnp.float32)
        packed = jnp.where(lane == 8 + slot, q_rows, packed)
    key_vec[...] = packed[:8].astype(jnp.int32)
    fetch = pltpu.make_async_copy(key_vec, keys, key_sem)
    fetch.start()
    fetch.wait()

    for h, out_ref in enumerate((keep_ref, send_ref)):

        def tile_step(i, carry, h=h, out_ref=out_ref):
            slot = i >> 1
            s = i & 1
            k4 = slot >> 1
            k2 = slot & 1
            key = keys[s, slot * 2 + h]
            inner = k2 * 4 + key
            start = pl.multiple_of(h * X_ROWS + s * TILE, 16)
            for b in range(2):
                place = b * 2 + k4
                match = jnp.int32(-1)
                for j in range(4):
                    match = jnp.where(keys[j, 8 + place] == inner, j, match)

                @pl.when((key >= 0) & (match >= 0))
                def _():
                    q_start = pl.multiple_of(match * TILE, 16)
                    out_ref[b] += jnp.dot(
                        x_buf[slot, pl.ds(start, TILE), :],
                        q_buf[place, pl.ds(q_start, TILE), :],
                        preferred_element_type=jnp.float32,
                    )

            @pl.when((key >= 0) & (layer == 0) & (y_hi == 0) & (k4 == 0) & (inner == z))
            def _():
                out_ref[core] -= 3.0 * x_buf[slot, pl.ds(start, TILE), :].astype(jnp.float32)

            return carry

        lax.fori_loop(0, 8, tile_step, 0)


def products(x_pieces, q_pieces):
    block = jax.ShapeDtypeStruct((2, TILE, TILE), jnp.float32)
    return pl.pallas_call(
        product_kernel,
        out_shape=(block, block),
        in_specs=[pl.BlockSpec(memory_space=pltpu.HBM)] * 16,
        out_specs=(pl.BlockSpec(memory_space=pltpu.VMEM),) * 2,
        scratch_shapes=[
            pltpu.VMEM((4, 2 * X_ROWS, TILE), jnp.bfloat16),
            pltpu.VMEM((4, Q_ROWS, TILE), jnp.bfloat16),
            pltpu.VMEM((8, 128), jnp.int32),
            pltpu.SMEM((8, 128), jnp.int32),
            pltpu.SemaphoreType.DMA((4,)),
            pltpu.SemaphoreType.DMA((4,)),
            pltpu.SemaphoreType.DMA,
        ],
        compiler_params=pltpu.CompilerParams(vmem_limit_bytes=24 * 1024 * 1024),
        cost_estimate=pl.CostEstimate(flops=2**28, bytes_accessed=5 * 2**20, transcendentals=0),
    )(*x_pieces, *q_pieces)


def on_device(matrix_tiles, matrix_where, matrix_count, square_tiles, square_where, square_count):
    layer_at = lax.axis_index("depth")
    row_at = lax.axis_index("row")
    col_at = lax.axis_index("col")
    x_live = jnp.arange(2, dtype=jnp.int32) < matrix_count[0]
    q_live = jnp.arange(4, dtype=jnp.int32) < square_count[0]
    x_key = jnp.where(x_live, matrix_where[:, 1] - layer_at * KDEP - col_at * XSLAB, -1)
    q_key = jnp.where(q_live, square_where[:, 0] - layer_at * KDEP - row_at * QSLAB, -1)

    permute = functools.partial(lax.ppermute, axis_name=ROW_COL)
    with jax.named_scope("pack"):
        own_q = with_keys(square_tiles, q_key)
        own_x = with_keys(matrix_tiles, x_key)
        both = jnp.concatenate([own_q, own_x], axis=0)
    with jax.named_scope("pair"):
        other = permute(both, perm=swap_pairs())
        other_q = other[:Q_ROWS]
        x_message = jnp.concatenate([own_x, other[Q_ROWS:]], axis=0)

    x_pieces = [x_message] + [None] * 7
    first = [own_q]
    shared = []
    second = other_q
    right = left = x_message
    for step in range(1, 5):
        with jax.named_scope("ring_square"):
            first.append(permute(first[-1], perm=y_pairs(step, 4)))
            if step < 4:
                second = permute(second, perm=y_pairs(step, 3))
                shared.append(permute(second, perm=share_pairs(step)))
        with jax.named_scope("ring_matrix"):
            right = permute(right, perm=z_pairs(step, 1))
            x_pieces[step] = right
            if step < 4:
                left = permute(left, perm=z_pairs(step, -1))
                x_pieces[8 - step] = left

    keep, send = products(x_pieces, first + shared)
    with jax.named_scope("pair_sum"):
        part = keep + permute(send, perm=swap_pairs())
    with jax.named_scope("scatter_sum"):
        groups = [
            [layer * 16 + y_hi * 8 + z for y_hi in range(2) for layer in range(8)] for z in range(8)
        ]
        shares = lax.all_to_all(
            part.reshape(16, TILE // 8, TILE), ("depth", "col"), 0, 0, axis_index_groups=groups
        )
        own = -0.5 * jnp.sum(shares, axis=0)
    with jax.named_scope("gather_rows"):
        spread = jnp.broadcast_to(own[None], (8, TILE // 8, TILE))
        return lax.all_to_all(spread, "depth", 0, 0).reshape(TILE, TILE)


def solution(mesh):
    in_specs = (
        P(("depth", "row", "col"), None, None),
        P(("depth", "row", "col"), None),
        P(("depth", "row", "col")),
        P(("depth", "row", "col"), None, None),
        P(("depth", "row", "col"), None),
        P(("depth", "row", "col")),
    )
    return jax.shard_map(
        on_device, mesh=mesh, in_specs=in_specs, out_specs=P("row", "col"), check_vma=False
    )
```

```python
import functools

import jax
import jax.numpy as jnp
from jax import lax
from jax.experimental import pallas as pl
from jax.experimental.pallas import tpu as pltpu
from jax.sharding import PartitionSpec as P

TILE = 256
META = 16
X_ROWS = 2 * TILE + META
Q_ROWS = 4 * TILE + META
KDEP = 64
XSLAB = 4
QSLAB = 8
ROW_COL = ("row", "col")


def flat(y, core, z):
    return ((y & 3) * 2 + core) * 16 + (y >> 2) * 8 + z


def places():
    return [(y, core, z) for y in range(8) for core in range(2) for z in range(8)]


def swap_pairs():
    return [(flat(y, core, z), flat(y, 1 - core, z)) for y, core, z in places()]


def z_pairs(step, way):
    pairs = []
    for y, core, z in places():
        origin = (z - way * (step - 1)) % 8
        if (origin >> 1 & 1) == core:
            pairs.append((flat(y, core, z), flat(y, core, (z + way) % 8)))
    return pairs


def needed(origin, target):
    return (origin >> 1 & 1) == (target >> 2)


def y_pairs(step, reach):
    pairs = []
    for y, core, z in places():
        way = 1 - 2 * core
        origin = (y - way * (step - 1)) % 8
        if any(needed(origin, (origin + way * t) % 8) for t in range(step, reach + 1)):
            pairs.append((flat(y, core, z), flat((y + way) % 8, core, z)))
    return pairs


def share_pairs(step):
    return [
        (flat(y, core, z), flat(y, 1 - core, z))
        for y, core, z in places()
        if needed((y - (1 - 2 * core) * step) % 8, y)
    ]


def with_keys(tiles, keys):
    count = tiles.shape[0]
    rows = jnp.pad(keys, (0, META - count), constant_values=-1)
    rows = jnp.broadcast_to(rows[:, None], (META, TILE)).astype(jnp.bfloat16)
    return jnp.concatenate([tiles.reshape(count * TILE, TILE), rows], axis=0)


def product_kernel(*refs):
    x_refs, q_refs = refs[:8], refs[8:16]
    keep_ref, send_ref, x_buf, q_buf, key_vec, keys, x_sem, q_sem, key_sem = refs[16:]
    layer = lax.axis_index("depth")
    row_at = lax.axis_index("row")
    col_at = lax.axis_index("col")
    core = row_at & 1
    z = col_at & 7
    y_hi = col_at >> 3
    y = y_hi * 4 + (row_at >> 1)
    for d in range(8):
        origin = (z - d) & 7
        slot = (origin >> 2) * 2 + (origin & 1)

        @pl.when(((origin >> 1) & 1) == core)
        def _():
            pltpu.make_async_copy(x_refs[d], x_buf.at[slot], x_sem.at[slot]).start()

        source = (y - (1 - 2 * core) * (d if d < 5 else 4 - d)) & 7
        place = (source >> 2) * 2 + (source & 1)

        @pl.when(((source >> 1) & 1) == y_hi)
        def _():
            pltpu.make_async_copy(q_refs[d], q_buf.at[place], q_sem.at[place]).start()

    keep_ref[...] = jnp.zeros_like(keep_ref)
    send_ref[...] = jnp.zeros_like(send_ref)
    for slot in range(4):
        pltpu.make_async_copy(x_refs[0], x_buf.at[slot], x_sem.at[slot]).wait()
        pltpu.make_async_copy(q_refs[0], q_buf.at[slot], q_sem.at[slot]).wait()

    lane = lax.broadcasted_iota(jnp.int32, (META, 128), 1)
    packed = jnp.zeros((META, 128), jnp.float32)
    for slot in range(4):
        for half in range(2):
            at = half * X_ROWS + 2 * TILE
            x_rows = x_buf[slot, at : at + META, :128].astype(jnp.float32)
            packed = jnp.where(lane == slot * 2 + half, x_rows, packed)
        q_rows = q_buf[slot, 4 * TILE :, :128].astype(jnp.float32)
        packed = jnp.where(lane == 8 + slot, q_rows, packed)
    key_vec[...] = packed[:8].astype(jnp.int32)
    fetch = pltpu.make_async_copy(key_vec, keys, key_sem)
    fetch.start()
    fetch.wait()

    for h, out_ref in enumerate((keep_ref, send_ref)):

        def tile_step(i, carry, h=h, out_ref=out_ref):
            slot = i >> 1
            s = i & 1
            k4 = slot >> 1
            k2 = slot & 1
            key = keys[s, slot * 2 + h]
            inner = k2 * 4 + key
            start = pl.multiple_of(h * X_ROWS + s * TILE, 16)
            for b in range(2):
                place = b * 2 + k4
                match = jnp.int32(-1)
                for j in range(4):
                    match = jnp.where(keys[j, 8 + place] == inner, j, match)

                @pl.when((key >= 0) & (match >= 0))
                def _():
                    q_start = pl.multiple_of(match * TILE, 16)
                    out_ref[:, b] += jnp.dot(
                        x_buf[slot, pl.ds(start, TILE), :],
                        q_buf[place, pl.ds(q_start, TILE), :],
                        preferred_element_type=jnp.float32,
                    ).reshape(8, TILE // 8, TILE)

            @pl.when((key >= 0) & (layer == 0) & (y_hi == 0) & (k4 == 0) & (inner == z))
            def _():
                diagonal = x_buf[slot, pl.ds(start, TILE), :].astype(jnp.float32)
                out_ref[:, core] -= 3.0 * diagonal.reshape(8, TILE // 8, TILE)

            return carry

        lax.fori_loop(0, 8, tile_step, 0)


def products(x_pieces, q_pieces):
    block = jax.ShapeDtypeStruct((8, 2, TILE // 8, TILE), jnp.float32)
    return pl.pallas_call(
        product_kernel,
        out_shape=(block, block),
        in_specs=[pl.BlockSpec(memory_space=pltpu.HBM)] * 16,
        out_specs=(pl.BlockSpec(memory_space=pltpu.VMEM),) * 2,
        scratch_shapes=[
            pltpu.VMEM((4, 2 * X_ROWS, TILE), jnp.bfloat16),
            pltpu.VMEM((4, Q_ROWS, TILE), jnp.bfloat16),
            pltpu.VMEM((8, 128), jnp.int32),
            pltpu.SMEM((8, 128), jnp.int32),
            pltpu.SemaphoreType.DMA((4,)),
            pltpu.SemaphoreType.DMA((4,)),
            pltpu.SemaphoreType.DMA,
        ],
        compiler_params=pltpu.CompilerParams(vmem_limit_bytes=24 * 1024 * 1024),
        cost_estimate=pl.CostEstimate(flops=2**28, bytes_accessed=5 * 2**20, transcendentals=0),
    )(*x_pieces, *q_pieces)


def on_device(matrix_tiles, matrix_where, matrix_count, square_tiles, square_where, square_count):
    layer_at = lax.axis_index("depth")
    row_at = lax.axis_index("row")
    col_at = lax.axis_index("col")
    x_live = jnp.arange(2, dtype=jnp.int32) < matrix_count[0]
    q_live = jnp.arange(4, dtype=jnp.int32) < square_count[0]
    x_key = jnp.where(x_live, matrix_where[:, 1] - layer_at * KDEP - col_at * XSLAB, -1)
    q_key = jnp.where(q_live, square_where[:, 0] - layer_at * KDEP - row_at * QSLAB, -1)

    permute = functools.partial(lax.ppermute, axis_name=ROW_COL)
    with jax.named_scope("pack"):
        own_q = with_keys(square_tiles, q_key)
        own_x = with_keys(matrix_tiles, x_key)
        both = jnp.concatenate([own_q, own_x], axis=0)
    with jax.named_scope("pair"):
        other = permute(both, perm=swap_pairs())
        other_q = other[:Q_ROWS]
        x_message = jnp.concatenate([own_x, other[Q_ROWS:]], axis=0)

    x_pieces = [x_message] + [None] * 7
    first = [own_q]
    shared = []
    second = other_q
    right = left = x_message
    for step in range(1, 5):
        with jax.named_scope("ring_square"):
            first.append(permute(first[-1], perm=y_pairs(step, 4)))
            if step < 4:
                second = permute(second, perm=y_pairs(step, 3))
                shared.append(permute(second, perm=share_pairs(step)))
        with jax.named_scope("ring_matrix"):
            right = permute(right, perm=z_pairs(step, 1))
            x_pieces[step] = right
            if step < 4:
                left = permute(left, perm=z_pairs(step, -1))
                x_pieces[8 - step] = left

    keep, send = products(x_pieces, first + shared)
    with jax.named_scope("pair_sum"):
        part = keep + permute(send, perm=swap_pairs())
    with jax.named_scope("scatter_sum"):
        groups = [
            [layer * 16 + y_hi * 8 + z for layer in range(8) for y_hi in range(2)] for z in range(8)
        ]
        shares = lax.all_to_all(
            part.reshape(16, TILE // 8, TILE), ("depth", "col"), 0, 0, axis_index_groups=groups
        )
        own = -0.5 * jnp.sum(shares, axis=0)
    with jax.named_scope("gather_rows"):
        spread = jnp.broadcast_to(own[None], (8, TILE // 8, TILE))
        return lax.all_to_all(spread, "depth", 0, 0).reshape(TILE, TILE)


def solution(mesh):
    in_specs = (
        P(("depth", "row", "col"), None, None),
        P(("depth", "row", "col"), None),
        P(("depth", "row", "col")),
        P(("depth", "row", "col"), None, None),
        P(("depth", "row", "col"), None),
        P(("depth", "row", "col")),
    )
    return jax.shard_map(
        on_device, mesh=mesh, in_specs=in_specs, out_specs=P("row", "col"), check_vma=False
    )
```
